256 devices in a mesh: row: 64 (over x, z, core), snap: 4 (over y).
Axes of the slice: x: 4, y: 4, z: 8, core: 2. Of those that a mesh axis runs over, the one named last changes fastest.
Arguments:
- anomalies: float32 [131072, 4096], P('row', 'snap'), may hold values from -600 to 600, as said below
- start_basis: float32 [4096, 128], P('snap'), may hold values from -0.09375 to 0.09375
Outputs:
- space_basis: float32 [131072, 128], P('row')
- time_basis: float32 [4096, 128], P('snap')
The draws below stay inside these ranges and needn't reach their ends.
Inputs may be any that keep to these rules, and one draw needn't show every extreme that they name: `anomalies`: real values of order one times positive scales of grid points and snapshots.
All inputs are finite; a program needn't handle non-finite values.
Results may differ from the reference program's by a relative error of at most 0.000084.
Values sent between devices are 32-bit elements; how exact they have to be, the bound alone decides.
No kernel may reach another device: no remote copies, remote signals or barrier semaphores. Data moves between devices by JAX's collectives and lax.ppermute only.
A program may use at most 64 MiB of HBM per device.

```python
import math
import jax
import jax.numpy as jnp
from jax import lax

K = 128
ROWS = 131072
SNAPS = 4096


def draw_anomalies(key, part):
    key = jax.random.fold_in(key, 5)
    keys = jax.random.split(key, 5)
    values = jax.random.truncated_normal(keys[0], -6.0, 6.0, (ROWS, SNAPS), jnp.float32)
    row_span = math.log(10.0)
    row_scale = jnp.exp(jax.random.uniform(keys[3], (ROWS, 1), jnp.float32, 0.0, row_span))
    col_scale = jnp.exp(jax.random.uniform(keys[4], (1, SNAPS), jnp.float32, 0.0, math.log(10.0)))
    return values * row_scale * col_scale


def steps_of(key, extent, cuts, smallest, top_value):
    loudness, own = 1.0, jax.random.fold_in(key, 6)
    for axis_at, parts in cuts:
        draws = jnp.exp(jax.random.uniform(jax.random.fold_in(own, axis_at), (parts,), jnp.float32, smallest / len(cuts), top_value / len(cuts)))
        loudness = loudness * jnp.repeat(draws, extent[axis_at] // parts).reshape([-1 if axis == axis_at else 1 for axis in range(len(extent))])
    return loudness


def centred(rng, extent, deviation, limit, pieces=(), held_as=jnp.bfloat16):
    gain = steps_of(rng, extent, pieces, -0.22, 0.18) if pieces else 1.0
    array = jax.random.normal(rng, extent, jnp.float32) * deviation * gain
    return jnp.minimum(jnp.maximum(array, -limit), limit).astype(held_as)


def setup_inputs(seed: int = 0) -> dict:
    key_of = jax.random.split(jax.random.key(seed), 3)
    return {
        "anomalies": draw_anomalies(jax.random.fold_in(key_of[2], 71), 0),
        "start_basis": centred(key_of[1], (SNAPS, K), SNAPS ** -0.5, 0.09375, ((0, 4),), jnp.float32),
    }


def orthonormal(block):
    gram = jnp.dot(block.T.astype(jnp.float32), block.astype(jnp.float32), precision=lax.Precision.HIGHEST, preferred_element_type=jnp.float32)
    factor = jnp.linalg.cholesky(gram)
    return lax.linalg.triangular_solve(factor, block, left_side=False, lower=True, transpose_a=True)

def reference(anomalies, start_basis):
    sketch = jnp.dot(anomalies.astype(jnp.float32), start_basis.astype(jnp.float32), precision=lax.Precision.HIGHEST, preferred_element_type=jnp.float32)
    space_basis = orthonormal(sketch)
    back = jnp.dot(anomalies.T.astype(jnp.float32), space_basis.astype(jnp.float32), precision=lax.Precision.HIGHEST, preferred_element_type=jnp.float32)
    time_basis = orthonormal(back)
    return (space_basis, time_basis)
```

```python
import jax
import jax.numpy as jnp
from jax import lax
from jax.sharding import Mesh, PartitionSpec as P

HIGH = lax.Precision.HIGH
HIGHEST = lax.Precision.HIGHEST


def shifted(value, axis, shift):
    n = lax.axis_size(axis)
    return lax.ppermute(value, axis, [(i, (i + shift) % n) for i in range(n)])


def scatter_sum(value, axis):
    n = lax.axis_size(axis)
    pieces = value.reshape((n, value.shape[0] // n) + value.shape[1:])
    me = lax.axis_index(axis)
    total = lax.dynamic_index_in_dim(pieces, me, 0, keepdims=False)
    for shift in range(1, n):
        piece = lax.dynamic_index_in_dim(pieces, (me + shift) % n, 0, keepdims=False)
        total = total + shifted(piece, axis, shift)
    return total


def gather(value, axis):
    n = lax.axis_size(axis)
    me = lax.axis_index(axis)
    rows = value.shape[0]
    whole = jnp.zeros((n * rows,) + value.shape[1:], value.dtype)
    whole = lax.dynamic_update_slice_in_dim(whole, value, me * rows, 0)
    for shift in range(1, n):
        piece = shifted(value, axis, shift)
        whole = lax.dynamic_update_slice_in_dim(whole, piece, ((me - shift) % n) * rows, 0)
    return whole


def exchange_sum(value, axis):
    n = lax.axis_size(axis)
    pieces = value.reshape((n, value.shape[0] // n) + value.shape[1:])
    return jnp.sum(lax.all_to_all(pieces, axis, 0, 0), 0)


def exchange_gather(value, axis):
    n = lax.axis_size(axis)
    copies = jnp.broadcast_to(value[None], (n,) + value.shape)
    got = lax.all_to_all(copies, axis, 0, 0)
    return got.reshape((n * value.shape[0],) + value.shape[1:])


def local_gram(block):
    return lax.dot_general(
        block, block, (((0,), (0,)), ((), ())), precision=HIGHEST, preferred_element_type=jnp.float32
    )


def apply_factor(gram, block):
    factor = jnp.linalg.cholesky(gram)
    return lax.linalg.triangular_solve(factor, block, left_side=False, lower=True, transpose_a=True)


def on_device(anomalies, start_basis):
    partial_sketch = jnp.dot(
        anomalies, start_basis, precision=HIGH, preferred_element_type=jnp.float32
    )
    sketch = gather(exchange_sum(partial_sketch, "y"), "y")
    partial_raw = lax.dot_general(
        anomalies,
        sketch,
        (((0,), (0,)), ((), ())),
        precision=HIGH,
        preferred_element_type=jnp.float32,
    )
    stacked = jnp.concatenate([partial_raw, local_gram(sketch)], 0)
    part = scatter_sum(stacked, "c")
    part = scatter_sum(part, "x")
    part = exchange_gather(exchange_sum(part, "z"), "z")
    whole = gather(gather(part, "x"), "c")
    snaps = anomalies.shape[1]
    raw, gram = whole[:snaps], whole[snaps:]
    space_basis = apply_factor(gram, sketch)
    back = apply_factor(gram, raw)
    gram_back = local_gram(back)
    gram_back = gram_back + sum(shifted(gram_back, "y", s) for s in (1, 2, 3))
    time_basis = apply_factor(gram_back, back)
    return (space_basis, time_basis)


def solution(mesh):
    split = Mesh(mesh.devices.reshape(4, 8, 2, 4), ("x", "z", "c", "y"))
    rows = ("x", "z", "c")
    return jax.shard_map(
        on_device,
        mesh=split,
        in_specs=(P(rows, "y"), P("y", None)),
        out_specs=(P(rows, None), P("y", None)),
        check_vma=False,
    )
```

```python
import functools

import jax
import jax.numpy as jnp
from jax import lax
from jax.experimental import pallas as pl
from jax.experimental.pallas import tpu as pltpu
from jax.sharding import Mesh, PartitionSpec as P

F32 = jnp.float32
BF16 = jnp.bfloat16
K = 128
NB = 16
VMEM_LIMIT = 24 * 2**20
HIGHEST = lax.Precision.HIGHEST
TN = (((0,), (0,)), ((), ()))
NT = (((1,), (1,)), ((), ()))
NN = (((1,), (0,)), ((), ()))


def dot(a, b, dims, precision=None):
    return lax.dot_general(a, b, dims, precision=precision, preferred_element_type=F32)


def scalars(*values):
    return jnp.stack([jnp.asarray(v, jnp.int32) for v in values])


def vmem():
    return pl.BlockSpec(memory_space=pltpu.VMEM)


def smem():
    return pl.BlockSpec(memory_space=pltpu.SMEM)


def params():
    return pltpu.CompilerParams(vmem_limit_bytes=VMEM_LIMIT)


def cost(flops, moved):
    return pl.CostEstimate(flops=flops, bytes_accessed=moved, transcendentals=0)


def halves(x):
    high = x.astype(BF16)
    return high, (x - high.astype(F32)).astype(BF16)


def thirds(x):
    high = x.astype(BF16).astype(F32)
    mid = (x - high).astype(BF16).astype(F32)
    return high, mid, x - high - mid


CHUNKS = 2


def start_copies(a_ref, buf_ref, sems, boxes):
    copies = []
    for i, (rows, cols, at) in enumerate(boxes):
        copy = pltpu.make_async_copy(a_ref.at[rows, cols], buf_ref.at[at, cols], sems.at[i])
        copy.start()
        copies.append(copy)
    return copies


def sketch_kernel(count, where_ref, a_ref, b_ref, *refs):
    o_refs, (w_ref, basis_ref, buf_ref, sems, basis_sem) = refs[:count], refs[count:]
    rows, snaps = o_refs[0].shape[0], a_ref.shape[1]
    step = rows // CHUNKS
    basis_copy = pltpu.make_async_copy(b_ref, basis_ref, basis_sem)
    basis_copy.start()
    boxes = []
    for i in range(count * CHUNKS):
        at = pl.multiple_of(where_ref[i // CHUNKS] * rows + i % CHUNKS * step, step)
        boxes.append((pl.ds(at, step), pl.ds(0, snaps), pl.ds(i * step, step)))
    copies = start_copies(a_ref, buf_ref, sems, boxes)
    basis_copy.wait()
    high, low = halves(basis_ref[...])
    w_ref[:, :K] = high
    w_ref[:, K:] = low
    for i in range(count * CHUNKS):
        copies[i].wait()
        a_high, a_low = halves(buf_ref[i * step : (i + 1) * step, :])
        both = dot(a_high, w_ref[...], NN)
        cross = dot(a_low, w_ref[:, :K], NN)
        at = i % CHUNKS * step
        o_refs[i // CHUNKS][at : at + step, :] = both[:, :K] + (both[:, K:] + cross)


def sketch_pieces(a, b, where):
    rows, snaps = a.shape[0] // 4, a.shape[1]
    count = len(where)
    return pl.pallas_call(
        functools.partial(sketch_kernel, count),
        in_specs=[smem()] + [pl.BlockSpec(memory_space=pltpu.HBM)] * 2,
        out_specs=[vmem()] * count,
        out_shape=[jax.ShapeDtypeStruct((rows, K), F32)] * count,
        scratch_shapes=[
            pltpu.VMEM((snaps, 2 * K), BF16),
            pltpu.VMEM((snaps, K), F32),
            pltpu.VMEM((count * rows, snaps), F32),
            pltpu.SemaphoreType.DMA((count * CHUNKS,)),
            pltpu.SemaphoreType.DMA,
        ],
        compiler_params=params(),
        cost_estimate=cost(6 * count * rows * snaps * K, 4 * (count * rows + K) * snaps),
        name="sketch_pieces",
    )(scalars(*where), a, b)


def raw_kernel(count, earlier, last, where_ref, a_ref, *refs):
    refs = list(refs)
    take = lambda n: [refs.pop(0) for _ in range(n)]
    s_refs = take(count)
    prev_refs = take(1 if earlier else 0)
    gram_refs = take(earlier if last else 0)
    rows, snaps = s_refs[0].shape[0], a_ref.shape[1]
    half = snaps // 2
    if last:
        o_ref, slot_ref, both_ref, buf_ref, sems = refs
    else:
        o_ref, *g_refs = take(1 + count)
        buf_ref, sems = refs
    boxes = []
    for j in range(2):
        for i in range(count):
            at = pl.multiple_of(where_ref[i] * rows, rows)
            boxes.append((pl.ds(at, rows), pl.ds(j * half, half), pl.ds(i * rows, rows)))
    copies = start_copies(a_ref, buf_ref, sems, boxes)
    for i in range(count):
        s = s_refs[i][...]
        gram = dot(s, s, TN, HIGHEST)
        if last:
            slot_ref[where_ref[i]] = gram
        else:
            g_refs[i][...] = gram
    if last:
        for i in range(earlier):
            slot_ref[where_ref[count + i]] = gram_refs[i][...]
        gram = ((slot_ref[0] + slot_ref[1]) + slot_ref[2]) + slot_ref[3]
        for j in range(8):
            o_ref[j // 4, j % 4, K:, :] = gram[16 * j : 16 * j + 16, :]
    for j in range(2):
        cols = slice(j * half, (j + 1) * half)
        for i in range(count):
            high, low = halves(s_refs[i][...])
            copies[j * count + i].wait()
            a_high, a_low = halves(buf_ref[i * rows : (i + 1) * rows, cols])
            both = dot(jnp.concatenate([high, low], 1), a_high, TN)
            cross = dot(high, a_low, TN)
            if last:
                both_ref[:, cols] = both
                both_ref[:K, cols] = both_ref[:K, cols] + (both_ref[K:, cols] + cross)
                for k in range(4):
                    at = slice(j * half + k * K, j * half + (k + 1) * K)
                    o_ref[j, k, :K, :] = prev_refs[0][:, at] + both_ref[:K, at]
            else:
                total = both[:K] + (both[K:] + cross)
                if i > 0:
                    total = o_ref[:, cols] + total
                elif earlier:
                    total = prev_refs[0][:, cols] + total
                o_ref[:, cols] = total


def raw_pieces(a, pieces, where, prev=None, grams=(), last=False):
    count, earlier = len(pieces), len(grams)
    rows, snaps = pieces[0].shape[0], a.shape[1]
    args = list(pieces) + ([prev] if earlier else []) + (list(grams) if last else [])
    scratch = [
        pltpu.VMEM((count * rows, snaps), F32),
        pltpu.SemaphoreType.DMA((2 * count,)),
    ]
    if last:
        out_shape = [jax.ShapeDtypeStruct((2, 4, K + 16, K), F32)]
        scratch = [pltpu.VMEM((4, K, K), F32), pltpu.VMEM((2 * K, snaps), F32)] + scratch
    else:
        out_shape = [jax.ShapeDtypeStruct((K, snaps), F32)]
        out_shape += [jax.ShapeDtypeStruct((K, K), F32)] * count
    return pl.pallas_call(
        functools.partial(raw_kernel, count, earlier, last),
        in_specs=[smem(), pl.BlockSpec(memory_space=pltpu.HBM)] + [vmem()] * len(args),
        out_specs=[vmem()] * len(out_shape),
        out_shape=out_shape,
        scratch_shapes=scratch,
        compiler_params=params(),
        cost_estimate=cost(6 * count * rows * snaps * K, 4 * (count * rows + 2 * K) * snaps),
        name="raw_pieces",
    )(where, a, *args)


def inverse_factor(w_ref, o_ref):
    lane = lax.broadcasted_iota(jnp.int32, (NB, K), 1)
    row = lax.broadcasted_iota(jnp.int32, (NB, K), 0)
    for lo in range(0, K, NB):
        hi = lo + NB
        block = w_ref[lo:hi, :]
        cols = [jnp.broadcast_to(block[:, lo + c : lo + c + 1], (NB, K)) for c in range(NB)]
        inv = [jnp.where(row == c, 1.0, 0.0) for c in range(NB)]
        for k in range(NB):
            pivot = cols[k][k : k + 1, :]
            r = lax.rsqrt(pivot)
            r = r * (1.5 - 0.5 * (pivot * r) * r)
            m = jnp.where(row > k, cols[k] * r, 0.0)
            for c in range(k + 1, NB):
                cols[c] = cols[c] - m * (cols[c][k : k + 1, :] * r)
            for c in range(k + 1):
                scaled = inv[c][k : k + 1, :] * r
                inv[c] = jnp.where(row == k, scaled, inv[c] - m * scaled)
        inside = (lane >= lo) & (lane < hi)
        block = jnp.where(inside, jnp.where(lane - lo == row, 1.0, 0.0), block)
        done = inv[0] * block[0:1, :]
        for c in range(1, NB):
            done = done + inv[c] * block[c : c + 1, :]
        o_ref[lo:hi, :] = jnp.where(lane < hi, done, 0.0)
        if hi < K:
            h, m, l = thirds(done)
            left = jnp.concatenate([h, h, m, h, l, m], 0).astype(BF16)
            right = jnp.concatenate([h, m, h, l, h, m], 0).astype(BF16)
            update = dot(left, right, TN)
            below = lax.broadcasted_iota(jnp.int32, (K - hi, K), 1)
            inside = (below >= lo) & (below < hi)
            w_ref[hi:, :] = jnp.where(inside, 0.0, w_ref[hi:, :]) - update[hi:, :]


def middle_kernel(where_ref, mine_ref, other_ref, inv_ref, back_ref, gram_ref, w_ref, raw_ref):
    x, c = where_ref[0], where_ref[1]
    for half, ref in ((c, mine_ref), (1 - c, other_ref)):
        for shift in range(4):
            at = half * 4 + (x + 4 - shift) % 4
            raw_ref[:, pl.ds(pl.multiple_of(at * K, K), K)] = ref[shift, :K, :]
            w_ref[pl.ds(pl.multiple_of(at * 16, 16), 16), :] = ref[shift, K:, :]
    inverse_factor(w_ref, inv_ref)
    back = dot(inv_ref[...], raw_ref[...], NN, HIGHEST)
    back_ref[...] = back
    gram_ref[...] = dot(back, back, NT, HIGHEST)


def middle(where, mine, other):
    snaps = 8 * K
    return pl.pallas_call(
        middle_kernel,
        in_specs=[smem(), vmem(), vmem()],
        out_specs=[vmem()] * 3,
        out_shape=[
            jax.ShapeDtypeStruct((K, K), F32),
            jax.ShapeDtypeStruct((K, snaps), F32),
            jax.ShapeDtypeStruct((K, K), F32),
        ],
        scratch_shapes=[pltpu.VMEM((K, K), F32), pltpu.VMEM((K, snaps), F32)],
        compiler_params=params(),
        cost_estimate=cost(24 * snaps * K * K, 8 * snaps * K),
        name="middle",
    )(where, mine, other)


def space_kernel(where_ref, inv_ref, back_t_ref, *refs):
    s_refs, (o_ref, back_ref) = refs[:4], refs[4:]
    rows = s_refs[0].shape[0]
    inv = inv_ref[...]
    for i, ref in enumerate(s_refs):
        at = pl.multiple_of(where_ref[i] * rows, rows)
        o_ref[pl.ds(at, rows), :] = dot(ref[...], inv, NT, HIGHEST)
    back_ref[...] = back_t_ref[...].T


def space(where, inv, back_t, pieces):
    rows = 4 * pieces[0].shape[0]
    snaps = back_t.shape[1]
    return pl.pallas_call(
        space_kernel,
        in_specs=[smem()] + [vmem()] * 6,
        out_specs=[vmem()] * 2,
        out_shape=[jax.ShapeDtypeStruct((rows, K), F32), jax.ShapeDtypeStruct((snaps, K), F32)],
        compiler_params=params(),
        cost_estimate=cost(12 * rows * K * K, 8 * (rows + snaps) * K),
        name="space",
    )(where, inv, back_t, *pieces)


def time_kernel(where_ref, back_ref, *refs):
    gram_refs, (o_ref, slot_ref, w_ref, inv_ref) = refs[:4], refs[4:]
    for i, ref in enumerate(gram_refs):
        slot_ref[where_ref[i]] = ref[...]
    w_ref[...] = ((slot_ref[0] + slot_ref[1]) + slot_ref[2]) + slot_ref[3]
    inverse_factor(w_ref, inv_ref)
    o_ref[...] = dot(back_ref[...], inv_ref[...], NT, HIGHEST)


def time_basis_of(where, back, grams):
    return pl.pallas_call(
        time_kernel,
        in_specs=[smem()] + [vmem()] * 5,
        out_specs=vmem(),
        out_shape=jax.ShapeDtypeStruct(back.shape, F32),
        scratch_shapes=[
            pltpu.VMEM((4, K, K), F32),
            pltpu.VMEM((K, K), F32),
            pltpu.VMEM((K, K), F32),
        ],
        compiler_params=params(),
        cost_estimate=cost(12 * back.shape[0] * K * K, 8 * back.shape[0] * K),
        name="time_basis",
    )(where, back, *grams)


def shifted(value, axis, shift):
    n = lax.axis_size(axis)
    return lax.ppermute(value, axis, [(i, (i + shift) % n) for i in range(n)])


def pick(value, index):
    return lax.dynamic_index_in_dim(value, index, 0, keepdims=False)


def on_device(anomalies, start_basis):
    x, c, y = lax.axis_index("x"), lax.axis_index("c"), lax.axis_index("y")
    owner = [y, (y + 3) % 4, (y + 2) % 4, (y + 1) % 4]

    anomalies = pltpu.with_memory_space_constraint(anomalies, pltpu.HBM)
    start_basis = pltpu.with_memory_space_constraint(start_basis, pltpu.HBM)
    (p2,) = sketch_pieces(anomalies, start_basis, [(y + 2) % 4])
    r2 = shifted(p2, "y", 2)
    p1, p3, p0 = sketch_pieces(anomalies, start_basis, [(y + 1) % 4, (y + 3) % 4, y])
    r1, r3 = shifted(p1, "y", 1), shifted(p3, "y", 3)
    own = p0 + r2 + r1 + r3
    s2, s1, s3 = (shifted(own, "y", shift) for shift in (2, 1, 3))
    raw, g0 = raw_pieces(anomalies, [own], scalars(owner[0]))
    raw, g1, g3 = raw_pieces(anomalies, [s1, s3], scalars(owner[1], owner[3]), raw, [g0])
    (stacked,) = raw_pieces(
        anomalies, [s2], scalars(owner[2], owner[0], owner[1], owner[3]), raw, [g0, g1, g3], True
    )

    part = pick(stacked, c) + shifted(pick(stacked, 1 - c), "c", 1)
    arrived = [shifted(pick(part, (x + shift) % 4), "x", shift) for shift in (2, 1, 3)]
    part = pick(part, x) + arrived[0] + arrived[1] + arrived[2]
    copies = jnp.broadcast_to(part[None], (8,) + part.shape)
    part = jnp.sum(lax.all_to_all(copies, "z", 0, 0), 0)
    e2, e1, e3 = (shifted(part, "x", shift) for shift in (2, 1, 3))
    mine = jnp.stack([part, e1, e2, e3])
    other = shifted(mine, "c", 1)
    inv, back_t, gram = middle(scalars(x, c), mine, other)

    t2, t1, t3 = (shifted(gram, "y", shift) for shift in (2, 1, 3))
    space_basis, back = space(scalars(*owner), inv, back_t, (own, s1, s2, s3))
    time_basis = time_basis_of(scalars(*owner), back, (gram, t1, t2, t3))
    return (space_basis, time_basis)


def solution(mesh):
    split = Mesh(mesh.devices.reshape(4, 8, 2, 4), ("x", "z", "c", "y"))
    rows = ("x", "z", "c")
    return jax.shard_map(
        on_device,
        mesh=split,
        in_specs=(P(rows, "y"), P("y", None)),
        out_specs=(P(rows, None), P("y", None)),
        check_vma=False,
    )
```

```python
import functools

import jax
import jax.numpy as jnp
from jax import lax
from jax.experimental import pallas as pl
from jax.experimental.pallas import tpu as pltpu
from jax.sharding import Mesh, PartitionSpec as P

F32 = jnp.float32
BF16 = jnp.bfloat16
K = 128
NB = 16
VMEM_LIMIT = 24 * 2**20
HIGHEST = lax.Precision.HIGHEST
TN = (((0,), (0,)), ((), ()))
NT = (((1,), (1,)), ((), ()))
NN = (((1,), (0,)), ((), ()))


def dot(a, b, dims, precision=None):
    return lax.dot_general(a, b, dims, precision=precision, preferred_element_type=F32)


def scalars(*values):
    return jnp.stack([jnp.asarray(v, jnp.int32) for v in values])


def vmem():
    return pl.BlockSpec(memory_space=pltpu.VMEM)


def smem():
    return pl.BlockSpec(memory_space=pltpu.SMEM)


def params():
    return pltpu.CompilerParams(vmem_limit_bytes=VMEM_LIMIT)


def cost(flops, moved):
    return pl.CostEstimate(flops=flops, bytes_accessed=moved, transcendentals=0)


def halves(x):
    high = x.astype(BF16)
    return high, (x - high.astype(F32)).astype(BF16)


def thirds(x):
    high = x.astype(BF16).astype(F32)
    mid = (x - high).astype(BF16).astype(F32)
    return high, mid, x - high - mid


def gram_of(s):
    high, mid, low = (part.astype(BF16) for part in thirds(s))
    all_three = jnp.concatenate([high, mid, low], 1)
    blocks = dot(all_three, jnp.concatenate([high, mid], 1), TN)
    cross = blocks[K : 2 * K, :K] + blocks[2 * K :, :K]
    return blocks[:K, :K] + ((cross + cross.T) + blocks[K : 2 * K, K:])


CHUNKS = 2


def start_copies(a_ref, buf_ref, sems, boxes):
    copies = []
    for i, (rows, cols, at) in enumerate(boxes):
        copy = pltpu.make_async_copy(a_ref.at[rows, cols], buf_ref.at[at, cols], sems.at[i])
        copy.start()
        copies.append(copy)
    return copies


def sketch_kernel(count, where_ref, a_ref, b_ref, *refs):
    o_refs, (w_ref, basis_ref, buf_ref, sems, basis_sem) = refs[:count], refs[count:]
    rows, snaps = o_refs[0].shape[0], a_ref.shape[1]
    step = rows // CHUNKS
    basis_copy = pltpu.make_async_copy(b_ref, basis_ref, basis_sem)
    basis_copy.start()
    boxes = []
    for i in range(count * CHUNKS):
        at = pl.multiple_of(where_ref[i // CHUNKS] * rows + i % CHUNKS * step, step)
        boxes.append((pl.ds(at, step), pl.ds(0, snaps), pl.ds(i * step, step)))
    copies = start_copies(a_ref, buf_ref, sems, boxes)
    basis_copy.wait()
    high, low = halves(basis_ref[...])
    w_ref[:, :K] = high
    w_ref[:, K:] = low
    for i in range(count * CHUNKS):
        copies[i].wait()
        a_high, a_low = halves(buf_ref[i * step : (i + 1) * step, :])
        both = dot(a_high, w_ref[...], NN)
        cross = dot(a_low, w_ref[:, :K], NN)
        at = i % CHUNKS * step
        o_refs[i // CHUNKS][at : at + step, :] = both[:, :K] + (both[:, K:] + cross)


def sketch_pieces(a, b, where):
    rows, snaps = a.shape[0] // 4, a.shape[1]
    count = len(where)
    return pl.pallas_call(
        functools.partial(sketch_kernel, count),
        in_specs=[smem()] + [pl.BlockSpec(memory_space=pltpu.HBM)] * 2,
        out_specs=[vmem()] * count,
        out_shape=[jax.ShapeDtypeStruct((rows, K), F32)] * count,
        scratch_shapes=[
            pltpu.VMEM((snaps, 2 * K), BF16),
            pltpu.VMEM((snaps, K), F32),
            pltpu.VMEM((count * rows, snaps), F32),
            pltpu.SemaphoreType.DMA((count * CHUNKS,)),
            pltpu.SemaphoreType.DMA,
        ],
        compiler_params=params(),
        cost_estimate=cost(6 * count * rows * snaps * K, 4 * (count * rows + K) * snaps),
        name="sketch_pieces",
    )(scalars(*where), a, b)


def own_kernel(where_ref, a_ref, s_ref, o_ref, g_ref, *refs):
    split_refs, (buf_ref, sems) = refs[:4], refs[4:]
    rows, snaps = s_ref.shape[0], a_ref.shape[1]
    boxes = []
    for i in range(4):
        at = pl.multiple_of(where_ref[i] * rows, rows)
        boxes.append((pl.ds(at, rows), pl.ds(0, snaps), pl.ds(i * rows, rows)))
    copies = start_copies(a_ref, buf_ref, sems, boxes)
    s = s_ref[...]
    g_ref[...] = gram_of(s)
    high, low = halves(s)
    both_s = jnp.concatenate([high, low], 1)
    copies[0].wait()
    for lo in range(0, snaps, 256):
        cols = slice(lo, lo + 256)
        a_high, a_low = halves(buf_ref[:rows, cols])
        both = dot(both_s, a_high, TN)
        cross = dot(high, a_low, TN)
        o_ref[:, cols] = both[:K] + (both[K:] + cross)
    for i in range(3):
        copies[i + 1].wait()
        a_high, a_low = halves(buf_ref[(i + 1) * rows : (i + 2) * rows, :])
        pair = split_refs[:2] if i < 2 else split_refs[2:]
        at = i % 2 * rows
        pair[0][at : at + rows, :] = a_high
        pair[1][at : at + rows, :] = a_low


def own_piece(a, s, where):
    rows, snaps = s.shape[0], a.shape[1]
    out_shape = [jax.ShapeDtypeStruct((K, snaps), F32), jax.ShapeDtypeStruct((K, K), F32)]
    out_shape += [jax.ShapeDtypeStruct((2 * rows, snaps), BF16)] * 2
    out_shape += [jax.ShapeDtypeStruct((rows, snaps), BF16)] * 2
    return pl.pallas_call(
        own_kernel,
        in_specs=[smem(), pl.BlockSpec(memory_space=pltpu.HBM), vmem()],
        out_specs=[vmem()] * 6,
        out_shape=out_shape,
        scratch_shapes=[pltpu.VMEM((4 * rows, snaps), F32), pltpu.SemaphoreType.DMA((4,))],
        compiler_params=params(),
        cost_estimate=cost(6 * rows * snaps * K, 4 * (4 * rows + 2 * K) * snaps),
        name="own_piece",
    )(where, a, s)


def two_kernel(high_ref, low_ref, s1_ref, s2_ref, prev_ref, o_ref, g1_ref, g2_ref):
    rows, snaps = s1_ref.shape[0], high_ref.shape[1]
    s = jnp.concatenate([s1_ref[...], s2_ref[...]], 0)
    g1_ref[...] = gram_of(s[:rows])
    g2_ref[...] = gram_of(s[rows:])
    high, low = halves(s)
    both_s = jnp.concatenate([high, low], 1)
    for lo in range(0, snaps, 256):
        cols = slice(lo, lo + 256)
        both = dot(both_s, high_ref[:, cols], TN)
        cross = dot(high, low_ref[:, cols], TN)
        o_ref[:, cols] = prev_ref[:, cols] + (both[:K] + (both[K:] + cross))


def two_pieces(high, low, s1, s2, prev):
    rows, snaps = s1.shape[0], high.shape[1]
    return pl.pallas_call(
        two_kernel,
        in_specs=[vmem()] * 5,
        out_specs=[vmem()] * 3,
        out_shape=[jax.ShapeDtypeStruct((K, snaps), F32)] + [jax.ShapeDtypeStruct((K, K), F32)] * 2,
        compiler_params=params(),
        cost_estimate=cost(12 * rows * snaps * K, 4 * (2 * rows + 2 * K) * snaps),
        name="two_pieces",
    )(high, low, s1, s2, prev)


def last_kernel(where_ref, high_ref, low_ref, s_ref, prev_ref, *refs):
    gram_refs, (o_ref, slot_ref, both_ref) = refs[:3], refs[3:]
    snaps = high_ref.shape[1]
    s = s_ref[...]
    for i in range(3):
        slot_ref[where_ref[i]] = gram_refs[i][...]
    slot_ref[where_ref[3]] = gram_of(s)
    gram = ((slot_ref[0] + slot_ref[1]) + slot_ref[2]) + slot_ref[3]
    for j in range(8):
        o_ref[j // 4, j % 4, K:, :] = gram[16 * j : 16 * j + 16, :]
    high, low = halves(s)
    both_s = jnp.concatenate([high, low], 1)
    for lo in range(0, snaps, 256):
        cols = slice(lo, lo + 256)
        both_ref[:, cols] = dot(both_s, high_ref[:, cols], TN)
        cross = dot(high, low_ref[:, cols], TN)
        both_ref[:K, cols] = both_ref[:K, cols] + (both_ref[K:, cols] + cross)
        for j in range(lo // K, lo // K + 2):
            at = slice(j * K, (j + 1) * K)
            o_ref[j // 4, j % 4, :K, :] = prev_ref[:, at] + both_ref[:K, at]


def last_piece(where, high, low, s, prev, grams):
    rows, snaps = s.shape[0], high.shape[1]
    return pl.pallas_call(
        last_kernel,
        in_specs=[smem()] + [vmem()] * 7,
        out_specs=vmem(),
        out_shape=jax.ShapeDtypeStruct((2, 4, K + 16, K), F32),
        scratch_shapes=[pltpu.VMEM((4, K, K), F32), pltpu.VMEM((2 * K, snaps), F32)],
        compiler_params=params(),
        cost_estimate=cost(6 * rows * snaps * K, 4 * (rows + 2 * K) * snaps),
        name="last_piece",
    )(where, high, low, s, prev, *grams)


def inverse_factor(w_ref, o_ref):
    lane = lax.broadcasted_iota(jnp.int32, (NB, K), 1)
    row = lax.broadcasted_iota(jnp.int32, (NB, K), 0)
    for lo in range(0, K, NB):
        hi = lo + NB
        block = w_ref[lo:hi, :]
        cols = [jnp.broadcast_to(block[:, lo + c : lo + c + 1], (NB, K)) for c in range(NB)]
        inv = [jnp.where(row == c, 1.0, 0.0) for c in range(NB)]
        for k in range(NB):
            pivot = cols[k][k : k + 1, :]
            r = lax.rsqrt(pivot)
            r = r * (1.5 - 0.5 * (pivot * r) * r)
            m = jnp.where(row > k, cols[k] * r, 0.0)
            for c in range(k + 1, NB):
                cols[c] = cols[c] - m * (cols[c][k : k + 1, :] * r)
            for c in range(k + 1):
                scaled = inv[c][k : k + 1, :] * r
                inv[c] = jnp.where(row == k, scaled, inv[c] - m * scaled)
        inside = (lane >= lo) & (lane < hi)
        block = jnp.where(inside, jnp.where(lane - lo == row, 1.0, 0.0), block)
        terms = [inv[c] * block[c : c + 1, :] for c in range(NB)]
        while len(terms) > 1:
            terms = [a + b for a, b in zip(terms[::2], terms[1::2])]
        done = terms[0]
        o_ref[lo:hi, :] = jnp.where(lane < hi, done, 0.0)
        if hi < K:
            h, m, l = thirds(done)
            left = jnp.concatenate([h, h, m, h, l, m], 0).astype(BF16)
            right = jnp.concatenate([h, m, h, l, h, m], 0).astype(BF16)
            update = dot(left, right, TN)
            below = lax.broadcasted_iota(jnp.int32, (K - hi, K), 1)
            inside = (below >= lo) & (below < hi)
            w_ref[hi:, :] = jnp.where(inside, 0.0, w_ref[hi:, :]) - update[hi:, :]


def middle_kernel(where_ref, mine_ref, other_ref, inv_ref, back_ref, gram_ref, w_ref, raw_ref):
    x, c = where_ref[0], where_ref[1]
    for half, ref in ((c, mine_ref), (1 - c, other_ref)):
        for shift in range(4):
            at = half * 4 + (x + 4 - shift) % 4
            raw_ref[:, pl.ds(pl.multiple_of(at * K, K), K)] = ref[shift, :K, :]
            w_ref[pl.ds(pl.multiple_of(at * 16, 16), 16), :] = ref[shift, K:, :]
    inverse_factor(w_ref, inv_ref)
    back = dot(inv_ref[...], raw_ref[...], NN, HIGHEST)
    back_ref[...] = back
    gram_ref[...] = dot(back, back, NT, HIGHEST)


def middle(where, mine, other):
    snaps = 8 * K
    return pl.pallas_call(
        middle_kernel,
        in_specs=[smem(), vmem(), vmem()],
        out_specs=[vmem()] * 3,
        out_shape=[
            jax.ShapeDtypeStruct((K, K), F32),
            jax.ShapeDtypeStruct((K, snaps), F32),
            jax.ShapeDtypeStruct((K, K), F32),
        ],
        scratch_shapes=[pltpu.VMEM((K, K), F32), pltpu.VMEM((K, snaps), F32)],
        compiler_params=params(),
        cost_estimate=cost(24 * snaps * K * K, 8 * snaps * K),
        name="middle",
    )(where, mine, other)


def space_kernel(where_ref, inv_ref, back_t_ref, *refs):
    s_refs, (o_ref, back_ref) = refs[:4], refs[4:]
    rows = s_refs[0].shape[0]
    inv = inv_ref[...]
    for i, ref in enumerate(s_refs):
        at = pl.multiple_of(where_ref[i] * rows, rows)
        o_ref[pl.ds(at, rows), :] = dot(ref[...], inv, NT, HIGHEST)
    back_ref[...] = back_t_ref[...].T


def space(where, inv, back_t, pieces):
    rows = 4 * pieces[0].shape[0]
    snaps = back_t.shape[1]
    return pl.pallas_call(
        space_kernel,
        in_specs=[smem()] + [vmem()] * 6,
        out_specs=[vmem()] * 2,
        out_shape=[jax.ShapeDtypeStruct((rows, K), F32), jax.ShapeDtypeStruct((snaps, K), F32)],
        compiler_params=params(),
        cost_estimate=cost(12 * rows * K * K, 8 * (rows + snaps) * K),
        name="space",
    )(where, inv, back_t, *pieces)


def time_kernel(where_ref, back_ref, *refs):
    gram_refs, (o_ref, slot_ref, w_ref, inv_ref) = refs[:4], refs[4:]
    for i, ref in enumerate(gram_refs):
        slot_ref[where_ref[i]] = ref[...]
    w_ref[...] = ((slot_ref[0] + slot_ref[1]) + slot_ref[2]) + slot_ref[3]
    inverse_factor(w_ref, inv_ref)
    o_ref[...] = dot(back_ref[...], inv_ref[...], NT, HIGHEST)


def time_basis_of(where, back, grams):
    return pl.pallas_call(
        time_kernel,
        in_specs=[smem()] + [vmem()] * 5,
        out_specs=vmem(),
        out_shape=jax.ShapeDtypeStruct(back.shape, F32),
        scratch_shapes=[
            pltpu.VMEM((4, K, K), F32),
            pltpu.VMEM((K, K), F32),
            pltpu.VMEM((K, K), F32),
        ],
        compiler_params=params(),
        cost_estimate=cost(12 * back.shape[0] * K * K, 8 * back.shape[0] * K),
        name="time_basis",
    )(where, back, *grams)


def shifted(value, axis, shift):
    n = lax.axis_size(axis)
    return lax.ppermute(value, axis, [(i, (i + shift) % n) for i in range(n)])


def pick(value, index):
    return lax.dynamic_index_in_dim(value, index, 0, keepdims=False)


def on_device(anomalies, start_basis):
    x, c, y = lax.axis_index("x"), lax.axis_index("c"), lax.axis_index("y")
    owner = [y, (y + 3) % 4, (y + 2) % 4, (y + 1) % 4]

    anomalies = pltpu.with_memory_space_constraint(anomalies, pltpu.HBM)
    start_basis = pltpu.with_memory_space_constraint(start_basis, pltpu.HBM)
    (p2,) = sketch_pieces(anomalies, start_basis, [(y + 2) % 4])
    r2 = shifted(p2, "y", 2)
    p1, p3 = sketch_pieces(anomalies, start_basis, [(y + 1) % 4, (y + 3) % 4])
    r1, r3 = shifted(p1, "y", 1), shifted(p3, "y", 3)
    (p0,) = sketch_pieces(anomalies, start_basis, [y])
    own = p0 + r2 + r1 + r3
    s2, s1, s3 = (shifted(own, "y", shift) for shift in (2, 1, 3))
    blocks = scalars(*owner)
    raw, g0, high, low, high3, low3 = own_piece(anomalies, own, blocks)
    raw, g1, g2 = two_pieces(high, low, s1, s2, raw)
    stacked = last_piece(blocks, high3, low3, s3, raw, (g0, g1, g2))

    part = pick(stacked, c) + shifted(pick(stacked, 1 - c), "c", 1)
    arrived = [shifted(pick(part, (x + shift) % 4), "x", shift) for shift in (2, 1, 3)]
    part = pick(part, x) + arrived[0] + arrived[1] + arrived[2]
    copies = jnp.broadcast_to(part[None], (8,) + part.shape)
    part = jnp.sum(lax.all_to_all(copies, "z", 0, 0), 0)
    e2, e1, e3 = (shifted(part, "x", shift) for shift in (2, 1, 3))
    mine = jnp.stack([part, e1, e2, e3])
    other = shifted(mine, "c", 1)
    inv, back_t, gram = middle(scalars(x, c), mine, other)

    t2, t1, t3 = (shifted(gram, "y", shift) for shift in (2, 1, 3))
    space_basis, back = space(scalars(*owner), inv, back_t, (own, s1, s2, s3))
    time_basis = time_basis_of(scalars(*owner), back, (gram, t1, t2, t3))
    return (space_basis, time_basis)


def solution(mesh):
    split = Mesh(mesh.devices.reshape(4, 8, 2, 4), ("x", "z", "c", "y"))
    rows = ("x", "z", "c")
    return jax.shard_map(
        on_device,
        mesh=split,
        in_specs=(P(rows, "y"), P("y", None)),
        out_specs=(P(rows, None), P("y", None)),
        check_vma=False,
    )
```

```python
import functools

import jax
import jax.numpy as jnp
from jax import lax
from jax.experimental import pallas as pl
from jax.experimental.pallas import tpu as pltpu
from jax.sharding import Mesh, PartitionSpec as P

F32 = jnp.float32
BF16 = jnp.bfloat16
K = 128
NB, SB = 32, 16
VMEM_LIMIT = 24 * 2**20
HIGHEST = lax.Precision.HIGHEST
TN = (((0,), (0,)), ((), ()))
NT = (((1,), (1,)), ((), ()))
NN = (((1,), (0,)), ((), ()))


def dot(a, b, dims, precision=None):
    return lax.dot_general(a, b, dims, precision=precision, preferred_element_type=F32)


def scalars(*values):
    return jnp.stack([jnp.asarray(v, jnp.int32) for v in values])


def vmem():
    return pl.BlockSpec(memory_space=pltpu.VMEM)


def smem():
    return pl.BlockSpec(memory_space=pltpu.SMEM)


def params():
    return pltpu.CompilerParams(vmem_limit_bytes=VMEM_LIMIT)


def cost(flops, moved):
    return pl.CostEstimate(flops=flops, bytes_accessed=moved, transcendentals=0)


def halves(x):
    high = x.astype(BF16)
    return high, (x - high.astype(F32)).astype(BF16)


def thirds(x):
    high = x.astype(BF16).astype(F32)
    mid = (x - high).astype(BF16).astype(F32)
    return high, mid, x - high - mid


def folded(blocks):
    cross = blocks[K : 2 * K, :K] + blocks[2 * K :, :K]
    return blocks[:K, :K] + ((cross + cross.T) + blocks[K : 2 * K, K:])


def gram_of(s):
    high, mid, low = (part.astype(BF16) for part in thirds(s))
    all_three = jnp.concatenate([high, mid, low], 1)
    return folded(dot(all_three, jnp.concatenate([high, mid], 1), TN))


CHUNKS = 2


def start_copies(a_ref, buf_ref, sems, boxes):
    copies = []
    for i, (rows, cols, at) in enumerate(boxes):
        copy = pltpu.make_async_copy(a_ref.at[rows, cols], buf_ref.at[at, cols], sems.at[i])
        copy.start()
        copies.append(copy)
    return copies


def sketch_kernel(count, where_ref, a_ref, b_ref, *refs):
    o_refs, (w_ref, basis_ref, buf_ref, sems, basis_sem) = refs[:count], refs[count:]
    rows, snaps = o_refs[0].shape[0], a_ref.shape[1]
    step = rows // CHUNKS
    basis_copy = pltpu.make_async_copy(b_ref, basis_ref, basis_sem)
    basis_copy.start()
    boxes = []
    for i in range(count * CHUNKS):
        at = pl.multiple_of(where_ref[i // CHUNKS] * rows + i % CHUNKS * step, step)
        boxes.append((pl.ds(at, step), pl.ds(0, snaps), pl.ds(i * step, step)))
    copies = start_copies(a_ref, buf_ref, sems, boxes)
    basis_copy.wait()
    high, low = halves(basis_ref[...])
    w_ref[:, :K] = high
    w_ref[:, K:] = low
    for i in range(count * CHUNKS):
        copies[i].wait()
        a_high, a_low = halves(buf_ref[i * step : (i + 1) * step, :])
        both = dot(a_high, w_ref[...], NN)
        cross = dot(a_low, w_ref[:, :K], NN)
        at = i % CHUNKS * step
        o_refs[i // CHUNKS][at : at + step, :] = both[:, :K] + (both[:, K:] + cross)


def sketch_pieces(a, b, where):
    rows, snaps = a.shape[0] // 4, a.shape[1]
    count = len(where)
    return pl.pallas_call(
        functools.partial(sketch_kernel, count),
        in_specs=[smem()] + [pl.BlockSpec(memory_space=pltpu.HBM)] * 2,
        out_specs=[vmem()] * count,
        out_shape=[jax.ShapeDtypeStruct((rows, K), F32)] * count,
        scratch_shapes=[
            pltpu.VMEM((snaps, 2 * K), BF16),
            pltpu.VMEM((snaps, K), F32),
            pltpu.VMEM((count * rows, snaps), F32),
            pltpu.SemaphoreType.DMA((count * CHUNKS,)),
            pltpu.SemaphoreType.DMA,
        ],
        compiler_params=params(),
        cost_estimate=cost(6 * count * rows * snaps * K, 4 * (count * rows + K) * snaps),
        name="sketch_pieces",
    )(scalars(*where), a, b)


def own_kernel(where_ref, a_ref, s_ref, o_ref, g_ref, *refs):
    split_refs, (buf_ref, sems) = refs[:4], refs[4:]
    rows, snaps = s_ref.shape[0], a_ref.shape[1]
    boxes = []
    for i in range(4):
        at = pl.multiple_of(where_ref[i] * rows, rows)
        boxes.append((pl.ds(at, rows), pl.ds(0, snaps), pl.ds(i * rows, rows)))
    copies = start_copies(a_ref, buf_ref, sems, boxes)
    s = s_ref[...]
    g_ref[...] = gram_of(s)
    high, low = halves(s)
    both_s = jnp.concatenate([high, low], 1)
    copies[0].wait()
    for lo in range(0, snaps, 256):
        cols = slice(lo, lo + 256)
        a_high, a_low = halves(buf_ref[:rows, cols])
        both = dot(both_s, a_high, TN)
        cross = dot(high, a_low, TN)
        o_ref[:, cols] = both[:K] + (both[K:] + cross)
    for i in range(3):
        copies[i + 1].wait()
        a_high, a_low = halves(buf_ref[(i + 1) * rows : (i + 2) * rows, :])
        pair = split_refs[:2] if i < 2 else split_refs[2:]
        at = i % 2 * rows
        pair[0][at : at + rows, :] = a_high
        pair[1][at : at + rows, :] = a_low


def own_piece(a, s, where):
    rows, snaps = s.shape[0], a.shape[1]
    out_shape = [jax.ShapeDtypeStruct((K, snaps), F32), jax.ShapeDtypeStruct((K, K), F32)]
    out_shape += [jax.ShapeDtypeStruct((2 * rows, snaps), BF16)] * 2
    out_shape += [jax.ShapeDtypeStruct((rows, snaps), BF16)] * 2
    return pl.pallas_call(
        own_kernel,
        in_specs=[smem(), pl.BlockSpec(memory_space=pltpu.HBM), vmem()],
        out_specs=[vmem()] * 6,
        out_shape=out_shape,
        scratch_shapes=[pltpu.VMEM((4 * rows, snaps), F32), pltpu.SemaphoreType.DMA((4,))],
        compiler_params=params(),
        cost_estimate=cost(6 * rows * snaps * K, 4 * (4 * rows + 2 * K) * snaps),
        name="own_piece",
    )(where, a, s)


def two_kernel(high_ref, low_ref, s1_ref, s2_ref, prev_ref, o_ref, g1_ref, g2_ref):
    rows, snaps = s1_ref.shape[0], high_ref.shape[1]
    s = jnp.concatenate([s1_ref[...], s2_ref[...]], 0)
    g1_ref[...] = gram_of(s[:rows])
    g2_ref[...] = gram_of(s[rows:])
    high, low = halves(s)
    both_s = jnp.concatenate([high, low], 1)
    for lo in range(0, snaps, 256):
        cols = slice(lo, lo + 256)
        both = dot(both_s, high_ref[:, cols], TN)
        cross = dot(high, low_ref[:, cols], TN)
        o_ref[:, cols] = prev_ref[:, cols] + (both[:K] + (both[K:] + cross))


def two_pieces(high, low, s1, s2, prev):
    rows, snaps = s1.shape[0], high.shape[1]
    return pl.pallas_call(
        two_kernel,
        in_specs=[vmem()] * 5,
        out_specs=[vmem()] * 3,
        out_shape=[jax.ShapeDtypeStruct((K, snaps), F32)] + [jax.ShapeDtypeStruct((K, K), F32)] * 2,
        compiler_params=params(),
        cost_estimate=cost(12 * rows * snaps * K, 4 * (2 * rows + 2 * K) * snaps),
        name="two_pieces",
    )(high, low, s1, s2, prev)


def last_kernel(high_ref, low_ref, s_ref, prev_ref, g0_ref, g1_ref, g2_ref, o_ref, both_ref):
    snaps = high_ref.shape[1]
    s = s_ref[...]
    gram = (g0_ref[...] + g2_ref[...]) + (g1_ref[...] + gram_of(s))
    for j in range(8):
        o_ref[j // 4, j % 4, K:, :] = gram[32 * (j % 4) : 32 * (j % 4) + 32, :]
    high, low = halves(s)
    both_s = jnp.concatenate([high, low], 1)
    for lo in range(0, snaps, 256):
        cols = slice(lo, lo + 256)
        both_ref[:, cols] = dot(both_s, high_ref[:, cols], TN)
        cross = dot(high, low_ref[:, cols], TN)
        both_ref[:K, cols] = both_ref[:K, cols] + (both_ref[K:, cols] + cross)
        for j in range(lo // K, lo // K + 2):
            at = slice(j * K, (j + 1) * K)
            o_ref[j // 4, j % 4, :K, :] = prev_ref[:, at] + both_ref[:K, at]


def last_piece(high, low, s, prev, grams):
    rows, snaps = s.shape[0], high.shape[1]
    return pl.pallas_call(
        last_kernel,
        in_specs=[vmem()] * 7,
        out_specs=vmem(),
        out_shape=jax.ShapeDtypeStruct((2, 4, K + 32, K), F32),
        scratch_shapes=[pltpu.VMEM((2 * K, snaps), F32)],
        compiler_params=params(),
        cost_estimate=cost(6 * rows * snaps * K, 4 * (rows + 2 * K) * snaps),
        name="last_piece",
    )(high, low, s, prev, *grams)


def inverse_factor(w_ref, o_ref):
    for lo in range(0, K, NB):
        hi = lo + NB
        rest = w_ref[lo:hi, :]
        tops = []
        for at in range(lo, hi, SB):
            lane = lax.broadcasted_iota(jnp.int32, (hi - at, K), 1)
            row = lax.broadcasted_iota(jnp.int32, (hi - at, K), 0)
            cols = [jnp.broadcast_to(rest[:, at + c : at + c + 1], rest.shape) for c in range(SB)]
            inside = (lane >= at) & (lane < at + SB)
            rest = jnp.where(inside, jnp.where(lane - at == row, 1.0, 0.0), rest)
            pivots = jnp.ones((SB, K), F32)
            for k in range(SB):
                pivot = cols[k][k : k + 1, :]
                pivots = jnp.where(row[:SB] == k, pivot, pivots)
                m = jnp.where(row > k, cols[k], 0.0) * (1.0 / pivot)
                for c in range(k + 1, SB):
                    cols[c] = cols[c] - m * cols[c][k : k + 1, :]
                rest = rest - m * rest[k : k + 1, :]
            r = lax.rsqrt(pivots)
            r = r * (1.5 - 0.5 * (pivots * r) * r)
            top = rest[:SB] * r
            rest = rest[SB:]
            lane = lane[:SB]
            o_ref[at : at + SB, :] = jnp.where(lane < at + SB, top, 0.0)
            tops.append(jnp.where((lane >= at + SB) & (lane < hi), 0.0, top))
        if hi < K:
            h, m, l = thirds(jnp.concatenate(tops, 0))
            left = jnp.concatenate([h, h, m, h, l, m], 0).astype(BF16)
            right = jnp.concatenate([h, m, h, l, h, m], 0).astype(BF16)
            update = dot(left, right, TN)
            below = lax.broadcasted_iota(jnp.int32, (K - hi, K), 1)
            inside = (below >= lo) & (below < hi)
            w_ref[hi:, :] = jnp.where(inside, 0.0, w_ref[hi:, :]) - update[hi:, :]


def factor_kernel(where_ref, quarters_ref, inv_ref, w_ref):
    for shift in range(4):
        at = (where_ref[0] + 4 - shift) % 4
        w_ref[pl.ds(pl.multiple_of(at * 32, 32), 32), :] = quarters_ref[shift]
    inverse_factor(w_ref, inv_ref)


def factor(where, quarters):
    return pl.pallas_call(
        factor_kernel,
        in_specs=[smem(), vmem()],
        out_specs=vmem(),
        out_shape=jax.ShapeDtypeStruct((K, K), F32),
        scratch_shapes=[pltpu.VMEM((K, K), F32)],
        compiler_params=params(),
        cost_estimate=cost(24 * 8 * K * K * K, 8 * K * K),
        name="factor",
    )(where, quarters)


def back_kernel(where_ref, inv_ref, mine_ref, other_ref, back_ref, gram_ref, raw_ref):
    x, c = where_ref[0], where_ref[1]
    for half, ref in ((c, mine_ref), (1 - c, other_ref)):
        for shift in range(4):
            at = half * 4 + (x + 4 - shift) % 4
            raw_ref[:, pl.ds(pl.multiple_of(at * K, K), K)] = ref[shift]
    inv_high, inv_low = halves(inv_ref[...])
    raw_high, raw_low = halves(raw_ref[...])
    back = dot(
        jnp.concatenate([inv_high, inv_high, inv_low], 1),
        jnp.concatenate([raw_high, raw_low, raw_high], 0),
        NN,
    )
    back_ref[...] = back
    high, mid, low = (part.astype(BF16) for part in thirds(back))
    gram_ref[...] = folded(
        dot(jnp.concatenate([high, mid, low], 0), jnp.concatenate([high, mid], 0), NT)
    )


def back_of(where, inv, mine, other):
    snaps = 8 * K
    return pl.pallas_call(
        back_kernel,
        in_specs=[smem(), vmem(), vmem(), vmem()],
        out_specs=[vmem()] * 2,
        out_shape=[jax.ShapeDtypeStruct((K, snaps), F32), jax.ShapeDtypeStruct((K, K), F32)],
        scratch_shapes=[pltpu.VMEM((K, snaps), F32)],
        compiler_params=params(),
        cost_estimate=cost(24 * snaps * K * K, 8 * snaps * K),
        name="back",
    )(where, inv, mine, other)


def space_kernel(where_ref, inv_ref, back_t_ref, *refs):
    s_refs, (o_ref, back_ref) = refs[:4], refs[4:]
    rows = s_refs[0].shape[0]
    inv = inv_ref[...]
    for i, ref in enumerate(s_refs):
        at = pl.multiple_of(where_ref[i] * rows, rows)
        o_ref[pl.ds(at, rows), :] = dot(ref[...], inv, NT, HIGHEST)
    high, low = halves(back_t_ref[...].T)
    back_ref[...] = jnp.concatenate([high, high, low], 1)


def space(where, inv, back_t, pieces):
    rows = 4 * pieces[0].shape[0]
    snaps = back_t.shape[1]
    return pl.pallas_call(
        space_kernel,
        in_specs=[smem()] + [vmem()] * 6,
        out_specs=[vmem()] * 2,
        out_shape=[jax.ShapeDtypeStruct((rows, K), F32), jax.ShapeDtypeStruct((snaps, 3 * K), BF16)],
        compiler_params=params(),
        cost_estimate=cost(12 * rows * K * K, 8 * (rows + snaps) * K),
        name="space",
    )(where, inv, back_t, *pieces)


def time_kernel(back_ref, g0_ref, g1_ref, g2_ref, g3_ref, o_ref, w_ref, inv_ref):
    w_ref[...] = (g0_ref[...] + g2_ref[...]) + (g1_ref[...] + g3_ref[...])
    inverse_factor(w_ref, inv_ref)
    high, low = halves(inv_ref[...])
    o_ref[...] = dot(back_ref[...], jnp.concatenate([high, low, high], 1), NT)


def time_basis_of(back, grams):
    return pl.pallas_call(
        time_kernel,
        in_specs=[vmem()] * 5,
        out_specs=vmem(),
        out_shape=jax.ShapeDtypeStruct((back.shape[0], K), F32),
        scratch_shapes=[pltpu.VMEM((K, K), F32)] * 2,
        compiler_params=params(),
        cost_estimate=cost(12 * back.shape[0] * K * K, 8 * back.shape[0] * K),
        name="time_basis",
    )(back, *grams)


def shifted(value, axis, shift):
    n = lax.axis_size(axis)
    return lax.ppermute(value, axis, [(i, (i + shift) % n) for i in range(n)])


def pick(value, index):
    return lax.dynamic_index_in_dim(value, index, 0, keepdims=False)


def on_device(anomalies, start_basis):
    x, c, y = lax.axis_index("x"), lax.axis_index("c"), lax.axis_index("y")
    owner = [y, (y + 3) % 4, (y + 2) % 4, (y + 1) % 4]

    anomalies = pltpu.with_memory_space_constraint(anomalies, pltpu.HBM)
    start_basis = pltpu.with_memory_space_constraint(start_basis, pltpu.HBM)
    (p2,) = sketch_pieces(anomalies, start_basis, [(y + 2) % 4])
    r2 = shifted(p2, "y", 2)
    p1, p3 = sketch_pieces(anomalies, start_basis, [(y + 1) % 4, (y + 3) % 4])
    r1, r3 = shifted(p1, "y", 1), shifted(p3, "y", 3)
    (p0,) = sketch_pieces(anomalies, start_basis, [y])
    own = p0 + r2 + r1 + r3
    s2, s1, s3 = (shifted(own, "y", shift) for shift in (2, 1, 3))
    blocks = scalars(*owner)
    raw, g0, high, low, high3, low3 = own_piece(anomalies, own, blocks)
    raw, g1, g2 = two_pieces(high, low, s1, s2, raw)
    stacked = last_piece(high3, low3, s3, raw, (g0, g1, g2))

    part = pick(stacked, c) + shifted(pick(stacked, 1 - c), "c", 1)
    arrived = [shifted(pick(part, (x + shift) % 4), "x", shift) for shift in (1, 3, 2)]
    part = pick(part, x) + arrived[0] + arrived[1] + arrived[2]
    part = part + lax.ppermute(part, "z", [(i, i ^ 1) for i in range(8)])
    z1, z3, z2 = (shifted(part, "z", shift) for shift in (2, 6, 4))
    part = (part + z2) + (z1 + z3)
    e1, e3, e2 = (shifted(part, "x", shift) for shift in (1, 3, 2))
    mine = jnp.stack([piece[:K] for piece in (part, e1, e2, e3)])
    quarters = jnp.stack([piece[K:] for piece in (part, e1, e2, e3)])
    other = shifted(mine, "c", 1)
    inv = factor(scalars(x), quarters)
    back_t, gram = back_of(scalars(x, c), inv, mine, other)

    t1, t3, t2 = (shifted(gram, "y", shift) for shift in (1, 3, 2))
    space_basis, back = space(scalars(*owner), inv, back_t, (own, s1, s2, s3))
    time_basis = time_basis_of(back, (gram, t1, t2, t3))
    return (space_basis, time_basis)


def solution(mesh):
    split = Mesh(mesh.devices.reshape(4, 8, 2, 4), ("x", "z", "c", "y"))
    rows = ("x", "z", "c")
    return jax.shard_map(
        on_device,
        mesh=split,
        in_specs=(P(rows, "y"), P("y", None)),
        out_specs=(P(rows, None), P("y", None)),
        check_vma=False,
    )
```

```python
import functools

import jax
import jax.numpy as jnp
from jax import lax
from jax.experimental import pallas as pl
from jax.experimental.pallas import tpu as pltpu
from jax.sharding import Mesh, PartitionSpec as P

F32 = jnp.float32
BF16 = jnp.bfloat16
K = 128
NB, SB = 32, 16
VMEM_LIMIT = 24 * 2**20
HIGHEST = lax.Precision.HIGHEST
TN = (((0,), (0,)), ((), ()))
NT = (((1,), (1,)), ((), ()))
NN = (((1,), (0,)), ((), ()))


def dot(a, b, dims, precision=None):
    return lax.dot_general(a, b, dims, precision=precision, preferred_element_type=F32)


def scalars(*values):
    return jnp.stack([jnp.asarray(v, jnp.int32) for v in values])


def vmem():
    return pl.BlockSpec(memory_space=pltpu.VMEM)


def smem():
    return pl.BlockSpec(memory_space=pltpu.SMEM)


def params():
    return pltpu.CompilerParams(vmem_limit_bytes=VMEM_LIMIT)


def cost(flops, moved):
    return pl.CostEstimate(flops=flops, bytes_accessed=moved, transcendentals=0)


def halves(x):
    high = x.astype(BF16)
    return high, (x - high.astype(F32)).astype(BF16)


def thirds(x):
    high = x.astype(BF16).astype(F32)
    mid = (x - high).astype(BF16).astype(F32)
    return high, mid, x - high - mid


def folded(blocks):
    cross = blocks[K : 2 * K, :K] + blocks[2 * K :, :K]
    return blocks[:K, :K] + ((cross + cross.T) + blocks[K : 2 * K, K:])


def gram_of(s):
    high, mid, low = (part.astype(BF16) for part in thirds(s))
    all_three = jnp.concatenate([high, mid, low], 1)
    return folded(dot(all_three, jnp.concatenate([high, mid], 1), TN))


CHUNKS = 2


def start_copies(a_ref, buf_ref, sems, boxes):
    copies = []
    for i, (rows, cols, at) in enumerate(boxes):
        copy = pltpu.make_async_copy(a_ref.at[rows, cols], buf_ref.at[at, cols], sems.at[i])
        copy.start()
        copies.append(copy)
    return copies


def sketch_kernel(count, where_ref, a_ref, b_ref, *refs):
    o_refs, (w_ref, basis_ref, buf_ref, sems, basis_sem) = refs[:count], refs[count:]
    rows, snaps = o_refs[0].shape[0], a_ref.shape[1]
    step = rows // CHUNKS
    basis_copy = pltpu.make_async_copy(b_ref, basis_ref, basis_sem)
    basis_copy.start()
    boxes = []
    for i in range(count * CHUNKS):
        at = pl.multiple_of(where_ref[i // CHUNKS] * rows + i % CHUNKS * step, step)
        boxes.append((pl.ds(at, step), pl.ds(0, snaps), pl.ds(i * step, step)))
    copies = start_copies(a_ref, buf_ref, sems, boxes)
    basis_copy.wait()
    high, low = halves(basis_ref[...])
    w_ref[:, :K] = high
    w_ref[:, K:] = low
    for i in range(count * CHUNKS):
        copies[i].wait()
        a_high, a_low = halves(buf_ref[i * step : (i + 1) * step, :])
        both = dot(a_high, w_ref[...], NN)
        cross = dot(a_low, w_ref[:, :K], NN)
        at = i % CHUNKS * step
        o_refs[i // CHUNKS][at : at + step, :] = both[:, :K] + (both[:, K:] + cross)


def sketch_pieces(a, b, where):
    rows, snaps = a.shape[0] // 4, a.shape[1]
    count = len(where)
    return pl.pallas_call(
        functools.partial(sketch_kernel, count),
        in_specs=[smem()] + [pl.BlockSpec(memory_space=pltpu.HBM)] * 2,
        out_specs=[vmem()] * count,
        out_shape=[jax.ShapeDtypeStruct((rows, K), F32)] * count,
        scratch_shapes=[
            pltpu.VMEM((snaps, 2 * K), BF16),
            pltpu.VMEM((snaps, K), F32),
            pltpu.VMEM((count * rows, snaps), F32),
            pltpu.SemaphoreType.DMA((count * CHUNKS,)),
            pltpu.SemaphoreType.DMA,
        ],
        compiler_params=params(),
        cost_estimate=cost(6 * count * rows * snaps * K, 4 * (count * rows + K) * snaps),
        name="sketch_pieces",
    )(scalars(*where), a, b)


def own_kernel(where_ref, a_ref, s_ref, o_ref, g_ref, *refs):
    split_refs, (buf_ref, sems) = refs[:4], refs[4:]
    rows, snaps = s_ref.shape[0], a_ref.shape[1]
    boxes = []
    for i in range(4):
        at = pl.multiple_of(where_ref[i] * rows, rows)
        boxes.append((pl.ds(at, rows), pl.ds(0, snaps), pl.ds(i * rows, rows)))
    copies = start_copies(a_ref, buf_ref, sems, boxes)
    s = s_ref[...]
    g_ref[...] = gram_of(s)
    high, low = halves(s)
    both_s = jnp.concatenate([high, low], 1)
    copies[0].wait()
    for lo in range(0, snaps, 256):
        cols = slice(lo, lo + 256)
        a_high, a_low = halves(buf_ref[:rows, cols])
        both = dot(both_s, a_high, TN)
        cross = dot(high, a_low, TN)
        o_ref[:, cols] = both[:K] + (both[K:] + cross)
    for i in range(3):
        copies[i + 1].wait()
        a_high, a_low = halves(buf_ref[(i + 1) * rows : (i + 2) * rows, :])
        pair = split_refs[:2] if i < 2 else split_refs[2:]
        at = i % 2 * rows
        pair[0][at : at + rows, :] = a_high
        pair[1][at : at + rows, :] = a_low


def own_piece(a, s, where):
    rows, snaps = s.shape[0], a.shape[1]
    out_shape = [jax.ShapeDtypeStruct((K, snaps), F32), jax.ShapeDtypeStruct((K, K), F32)]
    out_shape += [jax.ShapeDtypeStruct((2 * rows, snaps), BF16)] * 2
    out_shape += [jax.ShapeDtypeStruct((rows, snaps), BF16)] * 2
    return pl.pallas_call(
        own_kernel,
        in_specs=[smem(), pl.BlockSpec(memory_space=pltpu.HBM), vmem()],
        out_specs=[vmem()] * 6,
        out_shape=out_shape,
        scratch_shapes=[pltpu.VMEM((4 * rows, snaps), F32), pltpu.SemaphoreType.DMA((4,))],
        compiler_params=params(),
        cost_estimate=cost(6 * rows * snaps * K, 4 * (4 * rows + 2 * K) * snaps),
        name="own_piece",
    )(where, a, s)


def two_kernel(high_ref, low_ref, s1_ref, s2_ref, prev_ref, o_ref, g1_ref, g2_ref):
    rows, snaps = s1_ref.shape[0], high_ref.shape[1]
    s = jnp.concatenate([s1_ref[...], s2_ref[...]], 0)
    g1_ref[...] = gram_of(s[:rows])
    g2_ref[...] = gram_of(s[rows:])
    high, low = halves(s)
    both_s = jnp.concatenate([high, low], 1)
    for lo in range(0, snaps, 256):
        cols = slice(lo, lo + 256)
        both = dot(both_s, high_ref[:, cols], TN)
        cross = dot(high, low_ref[:, cols], TN)
        o_ref[:, cols] = prev_ref[:, cols] + (both[:K] + (both[K:] + cross))


def two_pieces(high, low, s1, s2, prev):
    rows, snaps = s1.shape[0], high.shape[1]
    return pl.pallas_call(
        two_kernel,
        in_specs=[vmem()] * 5,
        out_specs=[vmem()] * 3,
        out_shape=[jax.ShapeDtypeStruct((K, snaps), F32)] + [jax.ShapeDtypeStruct((K, K), F32)] * 2,
        compiler_params=params(),
        cost_estimate=cost(12 * rows * snaps * K, 4 * (2 * rows + 2 * K) * snaps),
        name="two_pieces",
    )(high, low, s1, s2, prev)


def last_kernel(high_ref, low_ref, s_ref, prev_ref, g0_ref, g1_ref, g2_ref, o_ref, both_ref):
    snaps = high_ref.shape[1]
    s = s_ref[...]
    gram = (g0_ref[...] + g2_ref[...]) + (g1_ref[...] + gram_of(s))
    for j in range(8):
        o_ref[j // 4, j % 4, K:, :] = gram[32 * (j % 4) : 32 * (j % 4) + 32, :]
    high, low = halves(s)
    both_s = jnp.concatenate([high, low], 1)
    for lo in range(0, snaps, 256):
        cols = slice(lo, lo + 256)
        both_ref[:, cols] = dot(both_s, high_ref[:, cols], TN)
        cross = dot(high, low_ref[:, cols], TN)
        both_ref[:K, cols] = both_ref[:K, cols] + (both_ref[K:, cols] + cross)
        for j in range(lo // K, lo // K + 2):
            at = slice(j * K, (j + 1) * K)
            o_ref[j // 4, j % 4, :K, :] = prev_ref[:, at] + both_ref[:K, at]


def last_piece(high, low, s, prev, grams):
    rows, snaps = s.shape[0], high.shape[1]
    return pl.pallas_call(
        last_kernel,
        in_specs=[vmem()] * 7,
        out_specs=vmem(),
        out_shape=jax.ShapeDtypeStruct((2, 4, K + 32, K), F32),
        scratch_shapes=[pltpu.VMEM((2 * K, snaps), F32)],
        compiler_params=params(),
        cost_estimate=cost(6 * rows * snaps * K, 4 * (rows + 2 * K) * snaps),
        name="last_piece",
    )(high, low, s, prev, *grams)


def inverse_factor(w_ref, o_ref):
    for lo in range(0, K, NB):
        hi = lo + NB
        rest = w_ref[lo:hi, :]
        tops = []
        for at in range(lo, hi, SB):
            lane = lax.broadcasted_iota(jnp.int32, (hi - at, K), 1)
            row = lax.broadcasted_iota(jnp.int32, (hi - at, K), 0)
            cols = [jnp.broadcast_to(rest[:, at + c : at + c + 1], rest.shape) for c in range(SB)]
            inside = (lane >= at) & (lane < at + SB)
            rest = jnp.where(inside, jnp.where(lane - at == row, 1.0, 0.0), rest)
            pivots = jnp.ones((SB, K), F32)
            for k in range(SB):
                pivot = cols[k][k : k + 1, :]
                pivots = jnp.where(row[:SB] == k, pivot, pivots)
                m = jnp.where(row > k, cols[k], 0.0) * (1.0 / pivot)
                for c in range(k + 1, SB):
                    cols[c] = cols[c] - m * cols[c][k : k + 1, :]
                rest = rest - m * rest[k : k + 1, :]
            r = lax.rsqrt(pivots)
            r = r * (1.5 - 0.5 * (pivots * r) * r)
            top = rest[:SB] * r
            rest = rest[SB:]
            lane = lane[:SB]
            o_ref[at : at + SB, :] = jnp.where(lane < at + SB, top, 0.0)
            tops.append(jnp.where((lane >= at + SB) & (lane < hi), 0.0, top))
        if hi < K:
            h, m, l = thirds(jnp.concatenate(tops, 0))
            left = jnp.concatenate([h, h, m, h, l, m], 0).astype(BF16)
            right = jnp.concatenate([h, m, h, l, h, m], 0).astype(BF16)
            update = dot(left, right, TN)
            below = lax.broadcasted_iota(jnp.int32, (K - hi, K), 1)
            inside = (below >= lo) & (below < hi)
            w_ref[hi:, :] = jnp.where(inside, 0.0, w_ref[hi:, :]) - update[hi:, :]


def factor_kernel(where_ref, quarters_ref, inv_ref, w_ref):
    for shift in range(4):
        at = (where_ref[0] + 4 - shift) % 4
        w_ref[pl.ds(pl.multiple_of(at * 32, 32), 32), :] = quarters_ref[shift]
    inverse_factor(w_ref, inv_ref)


def factor(where, quarters):
    return pl.pallas_call(
        factor_kernel,
        in_specs=[smem(), vmem()],
        out_specs=vmem(),
        out_shape=jax.ShapeDtypeStruct((K, K), F32),
        scratch_shapes=[pltpu.VMEM((K, K), F32)],
        compiler_params=params(),
        cost_estimate=cost(24 * 8 * K * K * K, 8 * K * K),
        name="factor",
    )(where, quarters)


def back_kernel(where_ref, inv_ref, mine_ref, other_ref, back_ref, gram_ref, raw_ref):
    x, c = where_ref[0], where_ref[1]
    for half, ref in ((c, mine_ref), (1 - c, other_ref)):
        for shift in range(4):
            at = half * 4 + (x + 4 - shift) % 4
            raw_ref[:, pl.ds(pl.multiple_of(at * K, K), K)] = ref[shift]
    inv_high, inv_low = halves(inv_ref[...])
    raw_high, raw_low = halves(raw_ref[...])
    back = dot(
        jnp.concatenate([inv_high, inv_high, inv_low], 1),
        jnp.concatenate([raw_high, raw_low, raw_high], 0),
        NN,
    )
    back_ref[...] = back
    high, mid, low = (part.astype(BF16) for part in thirds(back))
    gram_ref[...] = folded(
        dot(jnp.concatenate([high, mid, low], 0), jnp.concatenate([high, mid], 0), NT)
    )


def back_of(where, inv, mine, other):
    snaps = 8 * K
    return pl.pallas_call(
        back_kernel,
        in_specs=[smem(), vmem(), vmem(), vmem()],
        out_specs=[vmem()] * 2,
        out_shape=[jax.ShapeDtypeStruct((K, snaps), F32), jax.ShapeDtypeStruct((K, K), F32)],
        scratch_shapes=[pltpu.VMEM((K, snaps), F32)],
        compiler_params=params(),
        cost_estimate=cost(24 * snaps * K * K, 8 * snaps * K),
        name="back",
    )(where, inv, mine, other)


def space_kernel(where_ref, inv_ref, back_t_ref, *refs):
    s_refs, (o_ref, back_ref) = refs[:4], refs[4:]
    rows = s_refs[0].shape[0]
    inv = inv_ref[...]
    for i, ref in enumerate(s_refs):
        at = pl.multiple_of(where_ref[i] * rows, rows)
        o_ref[pl.ds(at, rows), :] = dot(ref[...], inv, NT, HIGHEST)
    high, low = halves(back_t_ref[...].T)
    back_ref[...] = jnp.concatenate([high, high, low], 1)


def space(where, inv, back_t, pieces):
    rows = 4 * pieces[0].shape[0]
    snaps = back_t.shape[1]
    return pl.pallas_call(
        space_kernel,
        in_specs=[smem()] + [vmem()] * 6,
        out_specs=[vmem()] * 2,
        out_shape=[jax.ShapeDtypeStruct((rows, K), F32), jax.ShapeDtypeStruct((snaps, 3 * K), BF16)],
        compiler_params=params(),
        cost_estimate=cost(12 * rows * K * K, 8 * (rows + snaps) * K),
        name="space",
    )(where, inv, back_t, *pieces)


def time_kernel(back_ref, g0_ref, g1_ref, g2_ref, g3_ref, o_ref, w_ref, inv_ref):
    w_ref[...] = (g0_ref[...] + g2_ref[...]) + (g1_ref[...] + g3_ref[...])
    inverse_factor(w_ref, inv_ref)
    high, low = halves(inv_ref[...])
    o_ref[...] = dot(back_ref[...], jnp.concatenate([high, low, high], 1), NT)


def time_basis_of(back, grams):
    return pl.pallas_call(
        time_kernel,
        in_specs=[vmem()] * 5,
        out_specs=vmem(),
        out_shape=jax.ShapeDtypeStruct((back.shape[0], K), F32),
        scratch_shapes=[pltpu.VMEM((K, K), F32)] * 2,
        compiler_params=params(),
        cost_estimate=cost(12 * back.shape[0] * K * K, 8 * back.shape[0] * K),
        name="time_basis",
    )(back, *grams)


def shifted(value, axis, shift):
    n = lax.axis_size(axis)
    return lax.ppermute(value, axis, [(i, (i + shift) % n) for i in range(n)])


def pick(value, index):
    return lax.dynamic_index_in_dim(value, index, 0, keepdims=False)


def on_device(anomalies, start_basis):
    x, c, y = lax.axis_index("x"), lax.axis_index("c"), lax.axis_index("y")
    owner = [y, (y + 3) % 4, (y + 2) % 4, (y + 1) % 4]

    anomalies = pltpu.with_memory_space_constraint(anomalies, pltpu.HBM)
    start_basis = pltpu.with_memory_space_constraint(start_basis, pltpu.HBM)
    (p2,) = sketch_pieces(anomalies, start_basis, [(y + 2) % 4])
    half = p2.shape[0] // 2
    top, bottom = shifted(p2[:half], "y", 1), shifted(p2[half:], "y", 3)
    p1, p3 = sketch_pieces(anomalies, start_basis, [(y + 1) % 4, (y + 3) % 4])
    p1 = jnp.concatenate([p1[:half] + top, p1[half:]], 0)
    p3 = jnp.concatenate([p3[:half], p3[half:] + bottom], 0)
    r1, r3 = shifted(p1, "y", 1), shifted(p3, "y", 3)
    (p0,) = sketch_pieces(anomalies, start_basis, [y])
    own = p0 + r1 + r3
    s2, s1, s3 = (shifted(own, "y", shift) for shift in (2, 1, 3))
    blocks = scalars(*owner)
    raw, g0, high, low, high3, low3 = own_piece(anomalies, own, blocks)
    raw, g1, g2 = two_pieces(high, low, s1, s2, raw)
    stacked = last_piece(high3, low3, s3, raw, (g0, g1, g2))

    part = pick(stacked, c) + shifted(pick(stacked, 1 - c), "c", 1)
    arrived = [shifted(pick(part, (x + shift) % 4), "x", shift) for shift in (1, 3, 2)]
    near = lax.optimization_barrier(pick(part, x) + arrived[0] + arrived[1])
    part = near + arrived[2]
    part = part + lax.ppermute(part, "z", [(i, i ^ 1) for i in range(8)])
    z2, z1, z3 = (shifted(part, "z", shift) for shift in (4, 2, 6))
    part = (part + z2) + (z1 + z3)
    e1, e3, e2 = (shifted(part, "x", shift) for shift in (1, 3, 2))
    mine = jnp.stack([piece[:K] for piece in (part, e1, e2, e3)])
    quarters = jnp.stack([piece[K:] for piece in (part, e1, e2, e3)])
    other = shifted(mine, "c", 1)
    inv = factor(scalars(x), quarters)
    back_t, gram = back_of(scalars(x, c), inv, mine, other)

    t1, t3, t2 = (shifted(gram, "y", shift) for shift in (1, 3, 2))
    space_basis, back = space(scalars(*owner), inv, back_t, (own, s1, s2, s3))
    time_basis = time_basis_of(back, (gram, t1, t2, t3))
    return (space_basis, time_basis)


def solution(mesh):
    split = Mesh(mesh.devices.reshape(4, 8, 2, 4), ("x", "z", "c", "y"))
    rows = ("x", "z", "c")
    return jax.shard_map(
        on_device,
        mesh=split,
        in_specs=(P(rows, "y"), P("y", None)),
        out_specs=(P(rows, None), P("y", None)),
        check_vma=False,
    )
```

```python
import functools

import jax
import jax.numpy as jnp
from jax import lax
from jax.experimental import pallas as pl
from jax.experimental.pallas import tpu as pltpu
from jax.sharding import Mesh, PartitionSpec as P

F32 = jnp.float32
BF16 = jnp.bfloat16
K = 128
NB, SB = 32, 16
VMEM_LIMIT = 24 * 2**20
HIGHEST = lax.Precision.HIGHEST
TN = (((0,), (0,)), ((), ()))
NT = (((1,), (1,)), ((), ()))
NN = (((1,), (0,)), ((), ()))


def dot(a, b, dims, precision=None):
    return lax.dot_general(a, b, dims, precision=precision, preferred_element_type=F32)


def scalars(*values):
    return jnp.stack([jnp.asarray(v, jnp.int32) for v in values])


def vmem():
    return pl.BlockSpec(memory_space=pltpu.VMEM)


def smem():
    return pl.BlockSpec(memory_space=pltpu.SMEM)


def params():
    return pltpu.CompilerParams(vmem_limit_bytes=VMEM_LIMIT)


def cost(flops, moved):
    return pl.CostEstimate(flops=flops, bytes_accessed=moved, transcendentals=0)


def halves(x):
    high = x.astype(BF16)
    return high, (x - high.astype(F32)).astype(BF16)


def thirds(x):
    high = x.astype(BF16).astype(F32)
    mid = (x - high).astype(BF16).astype(F32)
    return high, mid, x - high - mid


def folded(blocks):
    cross = blocks[K : 2 * K, :K] + blocks[2 * K :, :K]
    return blocks[:K, :K] + ((cross + cross.T) + blocks[K : 2 * K, K:])


def gram_of(s):
    high, mid, low = (part.astype(BF16) for part in thirds(s))
    all_three = jnp.concatenate([high, mid, low], 1)
    return folded(dot(all_three, jnp.concatenate([high, mid], 1), TN))


CHUNKS = 2


def start_copies(a_ref, buf_ref, sems, boxes):
    copies = []
    for i, (rows, cols, at) in enumerate(boxes):
        copy = pltpu.make_async_copy(a_ref.at[rows, cols], buf_ref.at[at, cols], sems.at[i])
        copy.start()
        copies.append(copy)
    return copies


def sketch_kernel(count, where_ref, a_ref, b_ref, *refs):
    o_refs, (w_ref, basis_ref, buf_ref, sems, basis_sem) = refs[:count], refs[count:]
    rows, snaps = o_refs[0].shape[0], a_ref.shape[1]
    step = rows // CHUNKS
    basis_copy = pltpu.make_async_copy(b_ref, basis_ref, basis_sem)
    basis_copy.start()
    boxes = []
    for i in range(count * CHUNKS):
        at = pl.multiple_of(where_ref[i // CHUNKS] * rows + i % CHUNKS * step, step)
        boxes.append((pl.ds(at, step), pl.ds(0, snaps), pl.ds(i * step, step)))
    copies = start_copies(a_ref, buf_ref, sems, boxes)
    basis_copy.wait()
    high, low = halves(basis_ref[...])
    w_ref[:, :K] = high
    w_ref[:, K:] = low
    for i in range(count * CHUNKS):
        copies[i].wait()
        a_high, a_low = halves(buf_ref[i * step : (i + 1) * step, :])
        both = dot(a_high, w_ref[...], NN)
        cross = dot(a_low, w_ref[:, :K], NN)
        at = i % CHUNKS * step
        o_refs[i // CHUNKS][at : at + step, :] = both[:, :K] + (both[:, K:] + cross)


def sketch_pieces(a, b, where):
    rows, snaps = a.shape[0] // 4, a.shape[1]
    count = len(where)
    return pl.pallas_call(
        functools.partial(sketch_kernel, count),
        in_specs=[smem()] + [pl.BlockSpec(memory_space=pltpu.HBM)] * 2,
        out_specs=[vmem()] * count,
        out_shape=[jax.ShapeDtypeStruct((rows, K), F32)] * count,
        scratch_shapes=[
            pltpu.VMEM((snaps, 2 * K), BF16),
            pltpu.VMEM((snaps, K), F32),
            pltpu.VMEM((count * rows, snaps), F32),
            pltpu.SemaphoreType.DMA((count * CHUNKS,)),
            pltpu.SemaphoreType.DMA,
        ],
        compiler_params=params(),
        cost_estimate=cost(6 * count * rows * snaps * K, 4 * (count * rows + K) * snaps),
        name="sketch_pieces",
    )(scalars(*where), a, b)


def own_kernel(where_ref, a_ref, s_ref, o_ref, g_ref, *refs):
    split_refs, (buf_ref, sems) = refs[:4], refs[4:]
    rows, snaps = s_ref.shape[0], a_ref.shape[1]
    boxes = []
    for i in range(4):
        at = pl.multiple_of(where_ref[i] * rows, rows)
        boxes.append((pl.ds(at, rows), pl.ds(0, snaps), pl.ds(i * rows, rows)))
    copies = start_copies(a_ref, buf_ref, sems, boxes)
    s = s_ref[...]
    g_ref[...] = gram_of(s)
    high, low = halves(s)
    both_s = jnp.concatenate([high, low], 1)
    copies[0].wait()
    for lo in range(0, snaps, 256):
        cols = slice(lo, lo + 256)
        a_high, a_low = halves(buf_ref[:rows, cols])
        both = dot(both_s, a_high, TN)
        cross = dot(high, a_low, TN)
        o_ref[:, cols] = both[:K] + (both[K:] + cross)
    for i in range(3):
        copies[i + 1].wait()
        a_high, a_low = halves(buf_ref[(i + 1) * rows : (i + 2) * rows, :])
        pair = split_refs[:2] if i < 2 else split_refs[2:]
        at = i % 2 * rows
        pair[0][at : at + rows, :] = a_high
        pair[1][at : at + rows, :] = a_low


def own_piece(a, s, where):
    rows, snaps = s.shape[0], a.shape[1]
    out_shape = [jax.ShapeDtypeStruct((K, snaps), F32), jax.ShapeDtypeStruct((K, K), F32)]
    out_shape += [jax.ShapeDtypeStruct((2 * rows, snaps), BF16)] * 2
    out_shape += [jax.ShapeDtypeStruct((rows, snaps), BF16)] * 2
    return pl.pallas_call(
        own_kernel,
        in_specs=[smem(), pl.BlockSpec(memory_space=pltpu.HBM), vmem()],
        out_specs=[vmem()] * 6,
        out_shape=out_shape,
        scratch_shapes=[pltpu.VMEM((4 * rows, snaps), F32), pltpu.SemaphoreType.DMA((4,))],
        compiler_params=params(),
        cost_estimate=cost(6 * rows * snaps * K, 4 * (4 * rows + 2 * K) * snaps),
        name="own_piece",
    )(where, a, s)


def two_kernel(high_ref, low_ref, s1_ref, s2_ref, prev_ref, o_ref, g1_ref, g2_ref):
    rows, snaps = s1_ref.shape[0], high_ref.shape[1]
    s = jnp.concatenate([s1_ref[...], s2_ref[...]], 0)
    g1_ref[...] = gram_of(s[:rows])
    g2_ref[...] = gram_of(s[rows:])
    high, low = halves(s)
    both_s = jnp.concatenate([high, low], 1)
    for lo in range(0, snaps, 256):
        cols = slice(lo, lo + 256)
        both = dot(both_s, high_ref[:, cols], TN)
        cross = dot(high, low_ref[:, cols], TN)
        o_ref[:, cols] = prev_ref[:, cols] + (both[:K] + (both[K:] + cross))


def two_pieces(high, low, s1, s2, prev):
    rows, snaps = s1.shape[0], high.shape[1]
    return pl.pallas_call(
        two_kernel,
        in_specs=[vmem()] * 5,
        out_specs=[vmem()] * 3,
        out_shape=[jax.ShapeDtypeStruct((K, snaps), F32)] + [jax.ShapeDtypeStruct((K, K), F32)] * 2,
        compiler_params=params(),
        cost_estimate=cost(12 * rows * snaps * K, 4 * (2 * rows + 2 * K) * snaps),
        name="two_pieces",
    )(high, low, s1, s2, prev)


def last_kernel(high_ref, low_ref, s_ref, prev_ref, g0_ref, g1_ref, g2_ref, o_ref, both_ref):
    snaps = high_ref.shape[1]
    s = s_ref[...]
    gram = (g0_ref[...] + g2_ref[...]) + (g1_ref[...] + gram_of(s))
    for j in range(8):
        o_ref[j // 4, j % 4, K:, :] = gram[32 * (j % 4) : 32 * (j % 4) + 32, :]
    high, low = halves(s)
    both_s = jnp.concatenate([high, low], 1)
    for lo in range(0, snaps, 256):
        cols = slice(lo, lo + 256)
        both_ref[:, cols] = dot(both_s, high_ref[:, cols], TN)
        cross = dot(high, low_ref[:, cols], TN)
        both_ref[:K, cols] = both_ref[:K, cols] + (both_ref[K:, cols] + cross)
        for j in range(lo // K, lo // K + 2):
            at = slice(j * K, (j + 1) * K)
            o_ref[j // 4, j % 4, :K, :] = prev_ref[:, at] + both_ref[:K, at]


def last_piece(high, low, s, prev, grams):
    rows, snaps = s.shape[0], high.shape[1]
    return pl.pallas_call(
        last_kernel,
        in_specs=[vmem()] * 7,
        out_specs=vmem(),
        out_shape=jax.ShapeDtypeStruct((2, 4, K + 32, K), F32),
        scratch_shapes=[pltpu.VMEM((2 * K, snaps), F32)],
        compiler_params=params(),
        cost_estimate=cost(6 * rows * snaps * K, 4 * (rows + 2 * K) * snaps),
        name="last_piece",
    )(high, low, s, prev, *grams)


def inverse_factor(w_ref, o_ref):
    for lo in range(0, K, NB):
        hi = lo + NB
        rest = w_ref[lo:hi, :]
        tops = []
        for at in range(lo, hi, SB):
            lane = lax.broadcasted_iota(jnp.int32, (hi - at, K), 1)
            row = lax.broadcasted_iota(jnp.int32, (hi - at, K), 0)
            cols = [jnp.broadcast_to(rest[:, at + c : at + c + 1], rest.shape) for c in range(SB)]
            inside = (lane >= at) & (lane < at + SB)
            rest = jnp.where(inside, jnp.where(lane - at == row, 1.0, 0.0), rest)
            pivots = jnp.ones((SB, K), F32)
            for k in range(SB):
                pivot = cols[k][k : k + 1, :]
                pivots = jnp.where(row[:SB] == k, pivot, pivots)
                m = jnp.where(row > k, cols[k], 0.0) * (1.0 / pivot)
                for c in range(k + 1, SB):
                    cols[c] = cols[c] - m * cols[c][k : k + 1, :]
                rest = rest - m * rest[k : k + 1, :]
            r = lax.rsqrt(pivots)
            r = r * (1.5 - 0.5 * (pivots * r) * r)
            top = rest[:SB] * r
            rest = rest[SB:]
            lane = lane[:SB]
            o_ref[at : at + SB, :] = jnp.where(lane < at + SB, top, 0.0)
            tops.append(jnp.where((lane >= at + SB) & (lane < hi), 0.0, top))
        if hi < K:
            h, m, l = thirds(jnp.concatenate(tops, 0))
            left = jnp.concatenate([h, h, m, h, l, m], 0).astype(BF16)
            right = jnp.concatenate([h, m, h, l, h, m], 0).astype(BF16)
            update = dot(left, right, TN)
            below = lax.broadcasted_iota(jnp.int32, (K - hi, K), 1)
            inside = (below >= lo) & (below < hi)
            w_ref[hi:, :] = jnp.where(inside, 0.0, w_ref[hi:, :]) - update[hi:, :]


def factor_kernel(where_ref, quarters_ref, inv_ref, w_ref):
    for shift in range(4):
        at = (where_ref[0] + 4 - shift) % 4
        w_ref[pl.ds(pl.multiple_of(at * 32, 32), 32), :] = quarters_ref[shift]
    inverse_factor(w_ref, inv_ref)


def factor(where, quarters):
    return pl.pallas_call(
        factor_kernel,
        in_specs=[smem(), vmem()],
        out_specs=vmem(),
        out_shape=jax.ShapeDtypeStruct((K, K), F32),
        scratch_shapes=[pltpu.VMEM((K, K), F32)],
        compiler_params=params(),
        cost_estimate=cost(24 * 8 * K * K * K, 8 * K * K),
        name="factor",
    )(where, quarters)


def back_kernel(where_ref, inv_ref, mine_ref, other_ref, back_ref, gram_ref, raw_ref):
    x, c = where_ref[0], where_ref[1]
    for half, ref in ((c, mine_ref), (1 - c, other_ref)):
        for shift in range(4):
            at = half * 4 + (x + 4 - shift) % 4
            raw_ref[:, pl.ds(pl.multiple_of(at * K, K), K)] = ref[shift]
    inv_high, inv_low = halves(inv_ref[...])
    raw_high, raw_low = halves(raw_ref[...])
    back = dot(
        jnp.concatenate([inv_high, inv_high, inv_low], 1),
        jnp.concatenate([raw_high, raw_low, raw_high], 0),
        NN,
    )
    back_ref[...] = back
    high, mid, low = (part.astype(BF16) for part in thirds(back))
    gram_ref[...] = folded(
        dot(jnp.concatenate([high, mid, low], 0), jnp.concatenate([high, mid], 0), NT)
    )


def back_of(where, inv, mine, other):
    snaps = 8 * K
    return pl.pallas_call(
        back_kernel,
        in_specs=[smem(), vmem(), vmem(), vmem()],
        out_specs=[vmem()] * 2,
        out_shape=[jax.ShapeDtypeStruct((K, snaps), F32), jax.ShapeDtypeStruct((K, K), F32)],
        scratch_shapes=[pltpu.VMEM((K, snaps), F32)],
        compiler_params=params(),
        cost_estimate=cost(24 * snaps * K * K, 8 * snaps * K),
        name="back",
    )(where, inv, mine, other)


def space_kernel(where_ref, inv_ref, back_t_ref, *refs):
    s_refs, (o_ref, back_ref) = refs[:4], refs[4:]
    rows = s_refs[0].shape[0]
    inv = inv_ref[...]
    for i, ref in enumerate(s_refs):
        at = pl.multiple_of(where_ref[i] * rows, rows)
        o_ref[pl.ds(at, rows), :] = dot(ref[...], inv, NT, HIGHEST)
    high, low = halves(back_t_ref[...].T)
    back_ref[...] = jnp.concatenate([high, high, low], 1)


def space(where, inv, back_t, pieces):
    rows = 4 * pieces[0].shape[0]
    snaps = back_t.shape[1]
    return pl.pallas_call(
        space_kernel,
        in_specs=[smem()] + [vmem()] * 6,
        out_specs=[vmem()] * 2,
        out_shape=[jax.ShapeDtypeStruct((rows, K), F32), jax.ShapeDtypeStruct((snaps, 3 * K), BF16)],
        compiler_params=params(),
        cost_estimate=cost(12 * rows * K * K, 8 * (rows + snaps) * K),
        name="space",
    )(where, inv, back_t, *pieces)


def time_kernel(back_ref, g0_ref, g1_ref, g2_ref, g3_ref, o_ref, w_ref, inv_ref, buf_ref, sems):
    w_ref[...] = (g0_ref[...] + g2_ref[...]) + (g1_ref[...] + g3_ref[...])
    inverse_factor(w_ref, inv_ref)
    high, low = halves(inv_ref[...])
    right = jnp.concatenate([high, low, high], 1)
    step = buf_ref.shape[0] // 4
    copies = []
    for i in range(4):
        at = pl.ds(i * step, step)
        buf_ref[at, :] = dot(back_ref[at, :], right, NT)
        copies.append(pltpu.make_async_copy(buf_ref.at[at, :], o_ref.at[at, :], sems.at[i]))
        copies[i].start()
    for copy in copies:
        copy.wait()


def time_basis_of(back, grams):
    return pl.pallas_call(
        time_kernel,
        in_specs=[vmem()] * 5,
        out_specs=pl.BlockSpec(memory_space=pltpu.HBM),
        out_shape=jax.ShapeDtypeStruct((back.shape[0], K), F32),
        scratch_shapes=[
            pltpu.VMEM((K, K), F32),
            pltpu.VMEM((K, K), F32),
            pltpu.VMEM((back.shape[0], K), F32),
            pltpu.SemaphoreType.DMA((4,)),
        ],
        compiler_params=params(),
        cost_estimate=cost(12 * back.shape[0] * K * K, 8 * back.shape[0] * K),
        name="time_basis",
    )(back, *grams)


def shifted(value, axis, shift):
    n = lax.axis_size(axis)
    return lax.ppermute(value, axis, [(i, (i + shift) % n) for i in range(n)])


def pick(value, index):
    return lax.dynamic_index_in_dim(value, index, 0, keepdims=False)


def on_device(anomalies, start_basis):
    x, c, y = lax.axis_index("x"), lax.axis_index("c"), lax.axis_index("y")
    owner = [y, (y + 3) % 4, (y + 2) % 4, (y + 1) % 4]

    anomalies = pltpu.with_memory_space_constraint(anomalies, pltpu.HBM)
    start_basis = pltpu.with_memory_space_constraint(start_basis, pltpu.HBM)
    (p2,) = sketch_pieces(anomalies, start_basis, [(y + 2) % 4])
    half = p2.shape[0] // 2
    top, bottom = shifted(p2[:half], "y", 1), shifted(p2[half:], "y", 3)
    p1, p3 = sketch_pieces(anomalies, start_basis, [(y + 1) % 4, (y + 3) % 4])
    p1 = jnp.concatenate([p1[:half] + top, p1[half:]], 0)
    p3 = jnp.concatenate([p3[:half], p3[half:] + bottom], 0)
    r1, r3 = shifted(p1, "y", 1), shifted(p3, "y", 3)
    (p0,) = sketch_pieces(anomalies, start_basis, [y])
    own = p0 + r1 + r3
    s2, s1, s3 = (shifted(own, "y", shift) for shift in (2, 1, 3))
    blocks = scalars(*owner)
    raw, g0, high, low, high3, low3 = own_piece(anomalies, own, blocks)
    raw, g1, g2 = two_pieces(high, low, s1, s2, raw)
    stacked = last_piece(high3, low3, s3, raw, (g0, g1, g2))

    part = pick(stacked, c) + shifted(pick(stacked, 1 - c), "c", 1)
    arrived = [shifted(pick(part, (x + shift) % 4), "x", shift) for shift in (1, 3, 2)]
    near = lax.optimization_barrier(pick(part, x) + arrived[0] + arrived[1])
    part = near + arrived[2]
    part = part + lax.ppermute(part, "z", [(i, i ^ 1) for i in range(8)])
    z2, z1, z3 = (shifted(part, "z", shift) for shift in (4, 2, 6))
    part = (part + z2) + (z1 + z3)
    e1, e3, e2 = (shifted(part, "x", shift) for shift in (1, 3, 2))
    mine = jnp.stack([piece[:K] for piece in (part, e1, e2, e3)])
    quarters = jnp.stack([piece[K:] for piece in (part, e1, e2, e3)])
    other = shifted(mine, "c", 1)
    inv = factor(scalars(x), quarters)
    back_t, gram = back_of(scalars(x, c), inv, mine, other)

    t1, t3, t2 = (shifted(gram, "y", shift) for shift in (1, 3, 2))
    space_basis, back = space(scalars(*owner), inv, back_t, (own, s1, s2, s3))
    time_basis = time_basis_of(back, (gram, t1, t2, t3))
    return (space_basis, time_basis)


def solution(mesh):
    split = Mesh(mesh.devices.reshape(4, 8, 2, 4), ("x", "z", "c", "y"))
    rows = ("x", "z", "c")
    return jax.shard_map(
        on_device,
        mesh=split,
        in_specs=(P(rows, "y"), P("y", None)),
        out_specs=(P(rows, None), P("y", None)),
        check_vma=False,
    )
```
